256 devices in a mesh: ctx: 16 (over y, z_hi, core), ch: 16 (over z_lo, x).
Axes of the slice: x: 4, y: 4, z: 8 (z_hi: 2, z_lo: 4; z = z_hi * 4 + z_lo), core: 2. Of those that a mesh axis runs over, the one named last changes fastest.
Arguments:
- streams: bfloat16 [3, 256, 524288], P(None, 'ch', 'ctx'), parts along dimension 1, may hold values from -6 to 6
- short_weight: bfloat16 [3, 256, 3], P(None, 'ch'), parts along dimension 1, may hold values from -3.5 to 3.5
- gate_bias: float32 [256], P('ch'), parts along dimension 0, may hold values from -1 to 1
- filter_spectrum: float32 [2, 256, 512, 2048], P(None, 'ch', None, 'ctx'), parts along dimension 1, may hold values from -6 to 6
Outputs:
- gated: bfloat16 [256, 524288], P('ch', 'ctx'), parts along dimension 0
The draws below stay inside these ranges and needn't reach their ends.
There are 16 independent parts, one for each index of `ch`. The reference program is written for one: setup_inputs(seed, part) draws one part's arguments, and reference() takes and returns one part's arrays. A program takes and returns all parts, laid end to end along the dimension named above; each array names one. Nothing has to cross between parts.
All inputs are finite; a program needn't handle non-finite values.
Results may differ from the reference program's by a relative error of at most 0.01.
Values may be sent and summed in bfloat16 or wider, within the bound.
No kernel may reach another device: no remote copies, remote signals or barrier semaphores. Data moves between devices by JAX's collectives and lax.ppermute only.
A program may use at most 192 MiB of HBM per device.

```python
import math
import jax
import jax.numpy as jnp

FACTOR_A = 2048
FACTOR_B = 512
SHORT_TAPS = 3
CHANNELS = 16
SEQUENCE = 524288


def shard_levels(rng, shape, pieces, low, top_value):
    def one(position, blocks):
        draws = jax.random.uniform(jax.random.fold_in(jax.random.fold_in(rng, 6), position), (blocks,), jnp.float32, low / len(pieces), top_value / len(pieces))
        return jnp.repeat(jnp.exp(draws), shape[position] // blocks).reshape((-1,) + (1,) * (len(shape) - position - 1))

    level = one(*pieces[0])
    for cut in pieces[1:]:
        level = level * one(*cut)
    return level


def gaussian(rng, shape, spread, bound, pieces=(), kind=jnp.bfloat16):
    values = spread * jax.random.normal(rng, shape, jnp.float32)
    if pieces:
        values = values * shard_levels(rng, shape, pieces, -0.22, 0.18)
    return jnp.clip(values, -bound, bound).astype(kind)


def setup_inputs(seed: int = 0, part: int = 0) -> dict:
    streams_of = jax.random.split(jax.random.key(seed), 5)
    part_keys = jax.random.split(jax.random.fold_in(streams_of[4], part), 5)
    streams = gaussian(part_keys[0], (3, CHANNELS, SEQUENCE), 1.0, 6.0, ((2, 16),))
    short_weight = gaussian(part_keys[1], (3, CHANNELS, SHORT_TAPS), SHORT_TAPS ** -0.5, 3.5)
    gate_bias = jnp.clip(jax.random.uniform(part_keys[2], (CHANNELS,), jnp.float32, -1.0, 1.0), -1.0, 1.0)
    filter_spectrum = gaussian(part_keys[3], (2, CHANNELS, FACTOR_B, FACTOR_A), 1.0, 6.0, ((3, 16),), jnp.float32)
    return {"streams": streams, "short_weight": short_weight, "gate_bias": gate_bias, "filter_spectrum": filter_spectrum}


def tables(row_start, row_count, col_start, col_count, size):
    row_index = row_start + jnp.arange(row_count, dtype=jnp.int32)[:, None]
    col_index = col_start + jnp.arange(col_count, dtype=jnp.int32)[None, :]
    turns = (row_index * col_index) % size
    angle = turns.astype(jnp.float32) * (2.0 * math.pi / size)
    return jnp.cos(angle), -jnp.sin(angle)


def featurize(padded, short_weight, length):
    weights = short_weight.astype(jnp.float32)
    tap_count = weights.shape[2]
    summed = jnp.zeros(padded.shape[:2] + (length,), jnp.float32)
    for offset in range(tap_count):
        begin = tap_count - 1 - offset
        summed = summed + weights[:, :, offset, None] * padded[:, :, begin:begin + length]
    return summed


def mult(form, left, right):
    return jnp.einsum(form, left.astype(jnp.float32), right.astype(jnp.float32))


def reference(streams, short_weight, gate_bias, filter_spectrum):
    half_rows = FACTOR_A // 2
    points = FACTOR_A * FACTOR_B
    padded = jnp.pad(streams.astype(jnp.float32), ((0, 0), (0, 0), (SHORT_TAPS - 1, 0)))
    mixed_streams = featurize(padded, short_weight, SEQUENCE)
    product = (mixed_streams[0] * mixed_streams[2]).astype(jnp.bfloat16)
    grid_rows = product.reshape(CHANNELS, half_rows, FACTOR_B)
    cos_a, sin_a = tables(0, half_rows, 0, FACTOR_A, FACTOR_A)
    cos_a = cos_a.astype(jnp.bfloat16)
    sin_a = sin_a.astype(jnp.bfloat16)
    twid_c, twid_s = tables(0, FACTOR_B, 0, FACTOR_A, points)
    first_real = mult("cab,ak->cbk", grid_rows, cos_a)
    first_imag = mult("cab,ak->cbk", grid_rows, sin_a)
    mid_real = (first_real * twid_c - first_imag * twid_s).astype(jnp.bfloat16)
    mid_imag = (first_real * twid_s + first_imag * twid_c).astype(jnp.bfloat16)
    cos_b, sin_b = tables(0, FACTOR_B, 0, FACTOR_B, FACTOR_B)
    cos_b = cos_b.astype(jnp.bfloat16)
    sin_b = sin_b.astype(jnp.bfloat16)
    spec_real = mult("cbk,bq->cqk", mid_real, cos_b) - mult("cbk,bq->cqk", mid_imag, sin_b)
    spec_imag = mult("cbk,bq->cqk", mid_real, sin_b) + mult("cbk,bq->cqk", mid_imag, cos_b)
    filter_real = filter_spectrum[0]
    filter_imag = filter_spectrum[1]
    prod_real = (spec_real * filter_real - spec_imag * filter_imag).astype(jnp.bfloat16)
    prod_imag = (spec_real * filter_imag + spec_imag * filter_real).astype(jnp.bfloat16)
    back_real = mult("cqk,qb->cbk", prod_real, cos_b) + mult("cqk,qb->cbk", prod_imag, sin_b)
    back_imag = mult("cqk,qb->cbk", prod_imag, cos_b) - mult("cqk,qb->cbk", prod_real, sin_b)
    turn_real = (back_real * twid_c + back_imag * twid_s).astype(jnp.bfloat16)
    turn_imag = (back_imag * twid_c - back_real * twid_s).astype(jnp.bfloat16)
    summed = mult("cbk,ak->cab", turn_real, cos_a) + mult("cbk,ak->cab", turn_imag, sin_a)
    conv_out = (summed * (1.0 / points)).astype(jnp.bfloat16).reshape(CHANNELS, SEQUENCE)
    result = mixed_streams[1] * (conv_out.astype(jnp.float32) + gate_bias.astype(jnp.float32)[:, None] * product.astype(jnp.float32))
    return result.astype(jnp.bfloat16)
```

```python
import math

import jax
import jax.numpy as jnp
from jax import lax
from jax.experimental import pallas as pl
from jax.experimental.pallas import tpu as pltpu
from jax.sharding import PartitionSpec as P

FACTOR_A = 2048
FACTOR_B = 512
SHORT_TAPS = 3
CHUNKS = 2
RING = 4
ROWS = 64
KEPT = 128


def send(block, target):
    return lax.ppermute(block, "ctx", [(i, target(i)) for i in range(16)])


def to_core(block):
    return send(block, lambda i: i ^ 1)


def to_far(block):
    return send(block, lambda i: i ^ 2)


def to_next(block):
    return send(block, lambda i: (i + 4) % 16)


def to_last(block):
    return send(block, lambda i: (i - 4) % 16)


def tables(row_index, col_index, size):
    turns = row_index[:, None] * col_index[None, :] % size
    angle = turns.astype(jnp.float32) * (2.0 * math.pi / size)
    return (jnp.cos(angle), -jnp.sin(angle))


def featurize(stream, rim, weights):
    stream = stream.astype(jnp.float32)
    rim = rim.astype(jnp.float32)
    padded = jnp.concatenate([rim, stream], axis=1)
    length = stream.shape[1]
    summed = weights[:, 0, None] * stream
    for offset in range(1, SHORT_TAPS):
        begin = SHORT_TAPS - 1 - offset
        summed = summed + weights[:, offset, None] * padded[:, begin : begin + length]
    return summed


def dot(left, right):
    return jnp.dot(left, right, preferred_element_type=jnp.float32)


PIECES = (128, 128, 128, 128, 128, 128, 64, 64, 64, 64)


def conv_kernel(*refs):
    count = len(PIECES)
    pieces = refs[:count]
    near_ref, other_ref, fwd_a, inv_a, fwd_b, inv_b, cos_ref, sin_ref = refs[count : count + 8]
    outs = refs[count + 8 :]
    half = 2 * KEPT
    block = jnp.concatenate([piece[0] for piece in pieces], axis=0)
    first = dot(fwd_a[...], block)
    cos, sin = cos_ref[...], sin_ref[...]
    real, imag = first[:half], first[half:]
    mid = jnp.concatenate(
        [
            (real * cos - imag * sin).astype(jnp.bfloat16),
            (real * sin + imag * cos).astype(jnp.bfloat16),
        ],
        axis=1,
    )
    spec = dot(mid, fwd_b[...])
    real, imag = spec[:, :FACTOR_B], spec[:, FACTOR_B:]
    filter_real = jnp.concatenate([near_ref[0, 0], other_ref[0, 0]], axis=0)
    filter_imag = jnp.concatenate([near_ref[1, 0], other_ref[1, 0]], axis=0)
    prod = jnp.concatenate(
        [
            (real * filter_real - imag * filter_imag).astype(jnp.bfloat16),
            (real * filter_imag + imag * filter_real).astype(jnp.bfloat16),
        ],
        axis=1,
    )
    back = dot(prod, inv_b[...])
    real, imag = back[:, :FACTOR_B], back[:, FACTOR_B:]
    turn = jnp.concatenate(
        [
            (real * cos + imag * sin).astype(jnp.bfloat16),
            (imag * cos - real * sin).astype(jnp.bfloat16),
        ],
        axis=0,
    )
    scale = 1.0 / (FACTOR_A * FACTOR_B)
    begin = 0
    for out in outs:
        rows = out.shape[1]
        out[0] = (dot(inv_a[begin : begin + rows], turn) * scale).astype(jnp.bfloat16)
        begin += rows


def convolve(pieces, near, other, shared):
    channels = pieces[0].shape[0]

    def channel(rows):
        return pl.BlockSpec((1, rows, FACTOR_B), lambda c: (c, 0, 0))

    spectrum = pl.BlockSpec((2, 1, KEPT, FACTOR_B), lambda c: (0, c, 0, 0))
    whole = [
        pl.BlockSpec(table.shape, lambda c: (0, 0), pipeline_mode=pl.Buffered(1)) for table in shared
    ]
    flops = channels * 8 * 512 * 512 * 1024
    return pl.pallas_call(
        conv_kernel,
        grid=(channels,),
        in_specs=[channel(rows) for rows in PIECES] + [spectrum, spectrum] + whole,
        out_specs=[channel(rows) for rows in PIECES],
        out_shape=[
            jax.ShapeDtypeStruct((channels, rows, FACTOR_B), jnp.bfloat16) for rows in PIECES
        ],
        compiler_params=pltpu.CompilerParams(vmem_limit_bytes=48 * 1024 * 1024),
        cost_estimate=pl.CostEstimate(
            flops=flops, bytes_accessed=channels * 3 * 1024 * 1024 + 8 * 1024 * 1024, transcendentals=0
        ),
    )(*pieces, near, other, *shared)


def gather_ring(block):
    below = to_next(block)
    above = to_last(block)
    far_low = to_next(below[:, :ROWS])
    far_high = to_last(above[:, ROWS:])
    return below, above, far_low, far_high


def joined(block, other):
    return block.astype(jnp.float32) + other.astype(jnp.float32)


def scatter_ring(own, below, above, far_low, far_high):
    low = joined(above[:, :ROWS], to_next(far_low)).astype(jnp.bfloat16)
    high = joined(below[:, ROWS:], to_last(far_high)).astype(jnp.bfloat16)
    from_below = to_next(jnp.concatenate([low, above[:, ROWS:]], axis=1))
    from_above = to_last(jnp.concatenate([below[:, :ROWS], high], axis=1))
    return joined(own, from_below) + from_above.astype(jnp.float32)


def per_device(streams, short_weight, gate_bias, filter_spectrum):
    place = lax.axis_index("ctx")
    core = place % 2
    channels = streams.shape[1]
    length = streams.shape[2]
    half = channels // 2
    rim = lax.ppermute(
        streams[:, :, length - (SHORT_TAPS - 1) :], "ctx", [(i, i + 1) for i in range(15)]
    )
    weights = short_weight.astype(jnp.float32)

    mine = lax.dynamic_slice_in_dim(filter_spectrum, core * half, half, axis=1)
    given = lax.dynamic_slice_in_dim(filter_spectrum, (1 - core) * half, half, axis=1)
    near = jnp.swapaxes(mine, 2, 3)
    other = jnp.swapaxes(to_core(given), 2, 3)

    product = (
        featurize(streams[0], rim[0], weights[0]) * featurize(streams[2], rim[2], weights[2])
    ).astype(jnp.bfloat16)
    rows = product.reshape(channels, ROWS, FACTOR_B)
    kept = lax.dynamic_slice_in_dim(rows, core * half, half, axis=0)
    passed = to_core(lax.dynamic_slice_in_dim(rows, (1 - core) * half, half, axis=0))
    pair = jnp.concatenate([kept, passed], axis=1)

    chip = place // 4
    slot = place % 4
    ring = jnp.stack([chip, (chip + 3) % RING, (chip + 1) % RING, (chip + 2) % RING])
    inner = jnp.stack([slot, slot ^ 1, slot ^ 2, slot ^ 3])
    device = (ring[:, None] * 4 + inner[None, :]).reshape(-1)
    row_index = (device[:, None] * ROWS + jnp.arange(ROWS, dtype=jnp.int32)[None, :]).reshape(-1)
    owner = jnp.stack([place, place ^ 1])
    freq_index = (owner[:, None] * KEPT + jnp.arange(KEPT, dtype=jnp.int32)[None, :]).reshape(-1)
    cols = jnp.arange(FACTOR_B, dtype=jnp.int32)
    cos_a, sin_a = tables(freq_index, row_index, FACTOR_A)
    fwd_a = jnp.concatenate([cos_a, sin_a], axis=0).astype(jnp.bfloat16)
    inv_a = fwd_a.T
    cos_b, sin_b = tables(cols, cols, FACTOR_B)
    cos_b = cos_b.astype(jnp.bfloat16)
    sin_b = sin_b.astype(jnp.bfloat16)
    fwd_b = jnp.block([[cos_b, sin_b], [-sin_b, cos_b]])
    inv_b = jnp.block([[cos_b, -sin_b], [sin_b, cos_b]])
    cos_t, sin_t = tables(freq_index, cols, FACTOR_A * FACTOR_B)
    shared = (fwd_a, inv_a, fwd_b, inv_b, cos_t, sin_t)

    step = half // CHUNKS
    convs = []
    for chunk in range(CHUNKS):
        part = slice(chunk * step, (chunk + 1) * step)
        own = pair[part]
        far = to_far(own)
        below_o, above_o, low_o, high_o = gather_ring(own)
        below_z, above_z, low_z, high_z = gather_ring(far)
        pieces = (own, far, below_o, below_z, above_o, above_z, low_o, high_o, low_z, high_z)
        outs = convolve(pieces, near[:, part], other[:, part], shared)
        convs.append(outs)
    sums = []
    for own, far, below_o, below_z, above_o, above_z, low_o, high_o, low_z, high_z in convs:
        far_sum = scatter_ring(far, below_z, above_z, low_z, high_z).astype(jnp.bfloat16)
        far_in = to_far(far_sum)
        own_sum = scatter_ring(own, below_o, above_o, low_o, high_o)
        sums.append((own_sum + far_in.astype(jnp.float32)).astype(jnp.bfloat16))
    conv = jnp.concatenate(sums, axis=0)
    mine = conv[:, :ROWS]
    passed = to_core(conv[:, ROWS:])
    conv = jnp.where(
        core == 0, jnp.concatenate([mine, passed], axis=0), jnp.concatenate([passed, mine], axis=0)
    )
    conv = conv.reshape(channels, length).astype(jnp.float32)
    gate = featurize(streams[1], rim[1], weights[1])
    return (gate * (conv + gate_bias[:, None] * product.astype(jnp.float32))).astype(jnp.bfloat16)


def solution(mesh):
    in_specs = (P(None, "ch", "ctx"), P(None, "ch", None), P("ch"), P(None, "ch", None, "ctx"))
    out_specs = P("ch", "ctx")
    return jax.shard_map(
        per_device, mesh=mesh, in_specs=in_specs, out_specs=out_specs, check_vma=False
    )
```

```python
import math

import jax
import jax.numpy as jnp
import numpy as np
from jax import lax
from jax.experimental import pallas as pl
from jax.experimental.pallas import tpu as pltpu
from jax.sharding import PartitionSpec as P

FACTOR_A = 2048
FACTOR_B = 512
SHORT_TAPS = 3
RING = 4
CHUNKS = (5, 3)
ROWS = 64
KEPT = 128
LANES = 128
COLUMNS = 16384


def send(block, target):
    return lax.ppermute(block, "ctx", [(i, target(i)) for i in range(16)])


def to_core(block):
    return send(block, lambda i: i ^ 1)


def to_far(block):
    return send(block, lambda i: i ^ 2)


def to_next(block):
    return send(block, lambda i: (i + 4) % 16)


def to_last(block):
    return send(block, lambda i: (i - 4) % 16)


def to_across(block):
    return send(block, lambda i: (i + 8) % 16)


def tied(*values):
    return lax.optimization_barrier(values)


def tables(row_index, col_index, size):
    turns = row_index[:, None] * col_index[None, :] % size
    angle = turns.astype(jnp.float32) * (2.0 * math.pi / size)
    return (jnp.cos(angle), -jnp.sin(angle))


def grid_tables():
    index = np.arange(FACTOR_B)
    angle = (index[:, None] * index[None, :] % FACTOR_B) * (2.0 * math.pi / FACTOR_B)
    return jnp.asarray(np.cos(angle), jnp.bfloat16), jnp.asarray(-np.sin(angle), jnp.bfloat16)


def featurize(ref, last_ref, rim_ref, weights):
    last = jnp.where(pl.program_id(0) == 0, rim_ref[0], last_ref[0]).astype(jnp.float32)
    block = ref[0].astype(jnp.float32)
    padded = jnp.concatenate([last, block], axis=1)
    summed = weights[:, 0:1] * block
    for tap in range(1, SHORT_TAPS):
        summed = summed + weights[:, tap : tap + 1] * pltpu.roll(padded, tap, 1)[:, LANES:]
    return summed


def product_kernel(weight_ref, first, first_last, first_rim, third, third_last, third_rim, out):
    left = featurize(first, first_last, first_rim, weight_ref[0].astype(jnp.float32))
    right = featurize(third, third_last, third_rim, weight_ref[2].astype(jnp.float32))
    out[...] = (left * right).astype(jnp.bfloat16)


def gate_kernel(weight_ref, second, second_last, second_rim, out):
    out[...] = featurize(second, second_last, second_rim, weight_ref[1].astype(jnp.float32))


def stream_specs(stream, channels):
    per_step = COLUMNS // LANES
    return [
        pl.BlockSpec((1, channels, COLUMNS), lambda j: (stream, 0, j)),
        pl.BlockSpec((1, channels, LANES), lambda j: (stream, 0, jnp.maximum(j * per_step - 1, 0))),
        pl.BlockSpec((1, channels, LANES), lambda j: (stream, 0, 0)),
    ]


def make_product(weights, streams, rim):
    channels, length = streams.shape[1:]
    return pl.pallas_call(
        product_kernel,
        grid=(length // COLUMNS,),
        in_specs=[pl.BlockSpec(weights.shape, lambda j: (0, 0, 0))]
        + stream_specs(0, channels)
        + stream_specs(2, channels),
        out_specs=pl.BlockSpec((channels, COLUMNS), lambda j: (0, j)),
        out_shape=jax.ShapeDtypeStruct((channels, length), jnp.bfloat16),
        compiler_params=pltpu.CompilerParams(vmem_limit_bytes=56 * 1024 * 1024),
        cost_estimate=pl.CostEstimate(
            flops=14 * channels * length, bytes_accessed=6 * channels * length, transcendentals=0
        ),
    )(weights, streams, streams, rim, streams, streams, rim)


def make_gate(weights, streams, rim):
    channels, length = streams.shape[1:]
    return pl.pallas_call(
        gate_kernel,
        grid=(length // COLUMNS,),
        in_specs=[pl.BlockSpec(weights.shape, lambda j: (0, 0, 0))] + stream_specs(1, channels),
        out_specs=pl.BlockSpec((channels, COLUMNS), lambda j: (0, j)),
        out_shape=jax.ShapeDtypeStruct((channels, length), jnp.float32),
        compiler_params=pltpu.CompilerParams(vmem_limit_bytes=56 * 1024 * 1024),
        cost_estimate=pl.CostEstimate(
            flops=7 * channels * length, bytes_accessed=6 * channels * length, transcendentals=0
        ),
    )(weights, streams, streams, rim)


def dot(left, right):
    return jnp.dot(left, right, preferred_element_type=jnp.float32)


AROUND = (128, 128, 64, 64, 128)
BESIDE = (128, 128, 128, 128)


def conv_kernel(count, core_ref, *refs):
    near, other, fwd_a, inv_a, cos_b, sin_b, cos_ref, sin_ref = refs[count : count + 8]
    half = 2 * KEPT
    block = jnp.concatenate([ref[0] for ref in refs[:count]], axis=0)
    first = dot(fwd_a[...], block)
    cos, sin = cos_ref[...], sin_ref[...]
    real, imag = first[:half], first[half:]
    mid_real = (real * cos - imag * sin).astype(jnp.bfloat16)
    mid_imag = (real * sin + imag * cos).astype(jnp.bfloat16)
    real = dot(mid_real, cos_b[...]) - dot(mid_imag, sin_b[...])
    imag = dot(mid_real, sin_b[...]) + dot(mid_imag, cos_b[...])
    filter_real = jnp.concatenate([near[0, 0].T, other[0, 0].T], axis=0)
    filter_imag = jnp.concatenate([near[1, 0].T, other[1, 0].T], axis=0)
    prod_real = (real * filter_real - imag * filter_imag).astype(jnp.bfloat16)
    prod_imag = (real * filter_imag + imag * filter_real).astype(jnp.bfloat16)
    real = dot(prod_real, cos_b[...]) + dot(prod_imag, sin_b[...])
    imag = dot(prod_imag, cos_b[...]) - dot(prod_real, sin_b[...])
    turn = jnp.concatenate(
        [
            (real * cos + imag * sin).astype(jnp.bfloat16),
            (imag * cos - real * sin).astype(jnp.bfloat16),
        ],
        axis=0,
    )
    scale = 1.0 / (FACTOR_A * FACTOR_B)
    begin = 0
    for out in refs[-count:]:
        rows = out.shape[1]
        out[0] = (dot(inv_a[begin : begin + rows], turn) * scale).astype(jnp.bfloat16)
        begin += rows


def convolve(core, pieces, begin, near, other, shared, around):
    half = near.shape[1] // 2
    channels = pieces[-1].shape[0]
    count = len(pieces)

    def spec(rows, first):
        return pl.BlockSpec((1, rows, FACTOR_B), lambda c, core: (first + c, 0, 0))

    specs = [spec(rows, begin) for rows in AROUND] + [spec(rows, 0) for rows in BESIDE]
    shapes = [(half, rows, FACTOR_B) for rows in AROUND]
    shapes += [(channels, rows, FACTOR_B) for rows in BESIDE]
    spectrum = (2, 1, FACTOR_B, KEPT)
    filters = pl.BlockSpec(spectrum, lambda c, core: (0, core[0] * half + begin + c, 0, 0))
    whole = [pl.BlockSpec(memory_space=pltpu.VMEM) for table in shared]
    inputs = (core, *pieces, near, other, *shared)
    return pl.pallas_call(
        lambda *refs: conv_kernel(count, *refs),
        grid_spec=pltpu.PrefetchScalarGridSpec(
            num_scalar_prefetch=1,
            grid=(channels,),
            in_specs=specs
            + [filters, filters]
            + whole
            + [pl.BlockSpec(memory_space=pl.ANY) for out in around],
            out_specs=specs,
        ),
        out_shape=[jax.ShapeDtypeStruct(shape, jnp.bfloat16) for shape in shapes],
        input_output_aliases={len(inputs) + i: i for i in range(len(around))},
        compiler_params=pltpu.CompilerParams(vmem_limit_bytes=56 * 1024 * 1024),
        cost_estimate=pl.CostEstimate(
            flops=(channels + 1) * 12 * 512 * 512 * 1024,
            bytes_accessed=channels * 3 * 1024 * 1024 + 4 * 1024 * 1024,
            transcendentals=0,
        ),
    )(*inputs, *around)


def gather_ring(far):
    return far, to_last(far), to_across(far), to_next(far)


def scatter_ring(outs):
    own, above, across, below = outs
    return own, to_next(above), to_across(across), to_last(below)


def total(parts):
    summed = joined(parts[0], parts[1])
    for part in parts[2:]:
        summed = summed + part.astype(jnp.float32)
    return summed


def relay(above, below):
    return to_last(above[:, :ROWS]), to_next(below[:, ROWS:])


def joined(block, other):
    return block.astype(jnp.float32) + other.astype(jnp.float32)


def scatter_far(outs):
    _, above, low, high, below = outs
    return to_next(low), to_last(high)


def scatter_near(outs, far):
    own, above, _, _, below = outs
    low = jnp.pad(far[0], ((0, 0), (0, ROWS), (0, 0)))
    high = jnp.pad(far[1], ((0, 0), (ROWS, 0), (0, 0)))
    from_below = to_next(joined(above, low).astype(jnp.bfloat16))
    from_above = to_last(joined(below, high).astype(jnp.bfloat16))
    return joined(own, from_below) + from_above.astype(jnp.float32)


def make_tables(place):
    chip = place // 4
    slot = place % 4
    ring = (chip + jnp.arange(RING, dtype=jnp.int32)) % RING
    here = ring[:, None] * 4 + jnp.stack([slot, slot ^ 1])[None, :]
    there = ring[:, None] * 4 + jnp.stack([slot ^ 2, slot ^ 3])[None, :]
    device = jnp.concatenate([here, there]).reshape(-1)
    row_index = (device[:, None] * ROWS + jnp.arange(ROWS, dtype=jnp.int32)[None, :]).reshape(-1)
    owner = jnp.stack([place, place ^ 1])
    freq_index = (owner[:, None] * KEPT + jnp.arange(KEPT, dtype=jnp.int32)[None, :]).reshape(-1)
    cols = jnp.arange(FACTOR_B, dtype=jnp.int32)
    cos_a, sin_a = tables(freq_index, row_index, FACTOR_A)
    fwd_a = jnp.concatenate([cos_a, sin_a], axis=0).astype(jnp.bfloat16)
    cos_b, sin_b = grid_tables()
    cos_t, sin_t = tables(freq_index, cols, FACTOR_A * FACTOR_B)
    return (fwd_a, fwd_a.T, cos_b, sin_b, cos_t, sin_t)


def per_device(streams, short_weight, gate_bias, filter_spectrum):
    place = lax.axis_index("ctx")
    core = place % 2
    channels = streams.shape[1]
    length = streams.shape[2]
    half = channels // 2
    rim = lax.ppermute(streams[:, :, length - LANES :], "ctx", [(i, i + 1) for i in range(15)])

    product = make_product(short_weight, streams, rim)
    rows = product.reshape(channels, ROWS, FACTOR_B)
    kept = lax.dynamic_slice_in_dim(rows, core * half, half, axis=0)
    passed = to_core(lax.dynamic_slice_in_dim(rows, (1 - core) * half, half, axis=0))
    later, passed, swapped = tied(place, passed, filter_spectrum)
    other = to_core(swapped)
    pair = jnp.concatenate([kept, passed], axis=1)

    which = core[None]
    step = CHUNKS[0]
    ring_pieces = len(AROUND)
    far0 = to_far(pair[:step])
    above_o, below_o = to_last(pair), to_next(pair)
    shared = make_tables(later)
    gate = make_gate(short_weight, streams, rim)
    above_o, below_o, shared, gate = tied(above_o, below_o, shared, gate)
    low_o, high_o = relay(above_o, below_o)
    pieces = gather_ring(far0)
    pair, low_o, high_o = tied(pair, low_o, high_o)
    around = (pair, above_o, low_o, high_o, below_o)
    far1 = to_far(pair[step:])

    *pieces, far1 = tied(*pieces, far1)
    outs0 = convolve(which, (*around, *pieces), 0, filter_spectrum, other, shared, ())
    pieces = gather_ring(far1)
    *pieces, outs0 = tied(*pieces, outs0)
    sum_z0 = total(scatter_ring(outs0[ring_pieces:])).astype(jnp.bfloat16)
    outs1 = convolve(
        which, (*around, *pieces), step, filter_spectrum, other, shared, outs0[:ring_pieces]
    )
    sum_z0, *outs1 = tied(sum_z0, *outs1)
    back0 = to_far(sum_z0)
    sum_z1 = total(scatter_ring(outs1[ring_pieces:])).astype(jnp.bfloat16)
    outs1 = outs1[:ring_pieces]
    low, high, sum_z1, back0 = tied(*scatter_far(outs1), sum_z1, back0)
    back1 = to_far(sum_z1)
    sum_o = scatter_near(outs1, (low, high))
    sums = [
        joined(sum_o[:step], back0).astype(jnp.bfloat16),
        joined(sum_o[step:], back1).astype(jnp.bfloat16),
    ]
    conv = jnp.concatenate(sums, axis=0)
    mine = conv[:, :ROWS]
    swapped = to_core(conv[:, ROWS:])
    conv = jnp.where(
        core == 0, jnp.concatenate([mine, swapped], axis=0), jnp.concatenate([swapped, mine], axis=0)
    )
    conv = conv.reshape(channels, length).astype(jnp.float32)
    direct = gate_bias[:, None] * product.astype(jnp.float32)
    return (gate * (conv + direct)).astype(jnp.bfloat16)


def solution(mesh):
    in_specs = (P(None, "ch", "ctx"), P(None, "ch", None), P("ch"), P(None, "ch", None, "ctx"))
    out_specs = P("ch", "ctx")
    return jax.shard_map(
        per_device, mesh=mesh, in_specs=in_specs, out_specs=out_specs, check_vma=False
    )
```

```python
import math

import jax
import jax.numpy as jnp
import numpy as np
from jax import lax
from jax.experimental import pallas as pl
from jax.experimental.pallas import tpu as pltpu
from jax.sharding import PartitionSpec as P

FACTOR_A = 2048
FACTOR_B = 512
SHORT_TAPS = 3
RING = 4
CHUNKS = (4, 4)
ROWS = 64
KEPT = 128
LANES = 128
COLUMNS = 16384


def send(block, target):
    return lax.ppermute(block, "ctx", [(i, target(i)) for i in range(16)])


def to_core(block):
    return send(block, lambda i: i ^ 1)


def to_far(block):
    return send(block, lambda i: i ^ 2)


def to_next(block):
    return send(block, lambda i: (i + 4) % 16)


def to_last(block):
    return send(block, lambda i: (i - 4) % 16)


def to_across(block):
    return send(block, lambda i: (i + 8) % 16)


def tied(*values):
    return lax.optimization_barrier(values)


def tables(row_index, col_index, size):
    turns = row_index[:, None] * col_index[None, :] % size
    angle = turns.astype(jnp.float32) * (2.0 * math.pi / size)
    return (jnp.cos(angle), -jnp.sin(angle))


def grid_tables():
    index = np.arange(FACTOR_B)
    angle = (index[:, None] * index[None, :] % FACTOR_B) * (2.0 * math.pi / FACTOR_B)
    return jnp.asarray(np.cos(angle), jnp.bfloat16), jnp.asarray(-np.sin(angle), jnp.bfloat16)


def featurize(ref, last_ref, rim_ref, weights):
    last = jnp.where(pl.program_id(0) == 0, rim_ref[0], last_ref[0]).astype(jnp.float32)
    block = ref[0].astype(jnp.float32)
    padded = jnp.concatenate([last, block], axis=1)
    summed = weights[:, 0:1] * block
    for tap in range(1, SHORT_TAPS):
        summed = summed + weights[:, tap : tap + 1] * pltpu.roll(padded, tap, 1)[:, LANES:]
    return summed


def product_kernel(weight_ref, first, first_last, first_rim, third, third_last, third_rim, out):
    left = featurize(first, first_last, first_rim, weight_ref[0].astype(jnp.float32))
    right = featurize(third, third_last, third_rim, weight_ref[2].astype(jnp.float32))
    out[...] = (left * right).astype(jnp.bfloat16)


def gate_kernel(weight_ref, second, second_last, second_rim, out):
    out[...] = featurize(second, second_last, second_rim, weight_ref[1].astype(jnp.float32))


def stream_specs(stream, channels):
    per_step = COLUMNS // LANES
    return [
        pl.BlockSpec((1, channels, COLUMNS), lambda j: (stream, 0, j)),
        pl.BlockSpec((1, channels, LANES), lambda j: (stream, 0, jnp.maximum(j * per_step - 1, 0))),
        pl.BlockSpec((1, channels, LANES), lambda j: (stream, 0, 0)),
    ]


def make_product(weights, streams, rim):
    channels, length = streams.shape[1:]
    return pl.pallas_call(
        product_kernel,
        grid=(length // COLUMNS,),
        in_specs=[pl.BlockSpec(weights.shape, lambda j: (0, 0, 0))]
        + stream_specs(0, channels)
        + stream_specs(2, channels),
        out_specs=pl.BlockSpec((channels, COLUMNS), lambda j: (0, j)),
        out_shape=jax.ShapeDtypeStruct((channels, length), jnp.bfloat16),
        compiler_params=pltpu.CompilerParams(vmem_limit_bytes=56 * 1024 * 1024),
        cost_estimate=pl.CostEstimate(
            flops=14 * channels * length, bytes_accessed=6 * channels * length, transcendentals=0
        ),
    )(weights, streams, streams, rim, streams, streams, rim)


def make_gate(weights, streams, rim):
    channels, length = streams.shape[1:]
    return pl.pallas_call(
        gate_kernel,
        grid=(length // COLUMNS,),
        in_specs=[pl.BlockSpec(weights.shape, lambda j: (0, 0, 0))] + stream_specs(1, channels),
        out_specs=pl.BlockSpec((channels, COLUMNS), lambda j: (0, j)),
        out_shape=jax.ShapeDtypeStruct((channels, length), jnp.float32),
        compiler_params=pltpu.CompilerParams(vmem_limit_bytes=56 * 1024 * 1024),
        cost_estimate=pl.CostEstimate(
            flops=7 * channels * length, bytes_accessed=6 * channels * length, transcendentals=0
        ),
    )(weights, streams, streams, rim)


def dot(left, right):
    return jnp.dot(left, right, preferred_element_type=jnp.float32)


AROUND = (128, 128, 64, 64, 128)
BESIDE = (128, 128, 128, 128)


def conv_kernel(count, core_ref, *refs):
    near, other, fwd_a, inv_a, cos_b, sin_b, cos_ref, sin_ref = refs[count : count + 8]
    half = 2 * KEPT
    block = jnp.concatenate([ref[0] for ref in refs[:count]], axis=0)
    first = dot(fwd_a[...], block)
    cos, sin = cos_ref[...], sin_ref[...]
    real, imag = first[:half], first[half:]
    mid_real = (real * cos - imag * sin).astype(jnp.bfloat16)
    mid_imag = (real * sin + imag * cos).astype(jnp.bfloat16)
    real = dot(mid_real, cos_b[...]) - dot(mid_imag, sin_b[...])
    imag = dot(mid_real, sin_b[...]) + dot(mid_imag, cos_b[...])
    filter_real = jnp.concatenate([near[0, 0].T, other[0, 0].T], axis=0)
    filter_imag = jnp.concatenate([near[1, 0].T, other[1, 0].T], axis=0)
    prod_real = (real * filter_real - imag * filter_imag).astype(jnp.bfloat16)
    prod_imag = (real * filter_imag + imag * filter_real).astype(jnp.bfloat16)
    real = dot(prod_real, cos_b[...]) + dot(prod_imag, sin_b[...])
    imag = dot(prod_imag, cos_b[...]) - dot(prod_real, sin_b[...])
    turn = jnp.concatenate(
        [
            (real * cos + imag * sin).astype(jnp.bfloat16),
            (imag * cos - real * sin).astype(jnp.bfloat16),
        ],
        axis=0,
    )
    scale = 1.0 / (FACTOR_A * FACTOR_B)
    begin = 0
    for out in refs[-count:]:
        rows = out.shape[1]
        out[0] = (dot(inv_a[begin : begin + rows], turn) * scale).astype(jnp.bfloat16)
        begin += rows


def convolve(core, pieces, begin, near, other, shared, around):
    half = near.shape[1] // 2
    channels = pieces[-1].shape[0]
    count = len(pieces)

    def spec(rows, first):
        return pl.BlockSpec((1, rows, FACTOR_B), lambda c, core: (first + c, 0, 0))

    specs = [spec(rows, begin) for rows in AROUND] + [spec(rows, 0) for rows in BESIDE]
    shapes = [(half, rows, FACTOR_B) for rows in AROUND]
    shapes += [(channels, rows, FACTOR_B) for rows in BESIDE]
    spectrum = (2, 1, FACTOR_B, KEPT)
    filters = pl.BlockSpec(spectrum, lambda c, core: (0, core[0] * half + begin + c, 0, 0))
    whole = [pl.BlockSpec(memory_space=pltpu.VMEM) for table in shared]
    inputs = (core, *pieces, near, other, *shared)
    return pl.pallas_call(
        lambda *refs: conv_kernel(count, *refs),
        grid_spec=pltpu.PrefetchScalarGridSpec(
            num_scalar_prefetch=1,
            grid=(channels,),
            in_specs=specs
            + [filters, filters]
            + whole
            + [pl.BlockSpec(memory_space=pl.ANY) for out in around],
            out_specs=specs,
        ),
        out_shape=[jax.ShapeDtypeStruct(shape, jnp.bfloat16) for shape in shapes],
        input_output_aliases={len(inputs) + i: i for i in range(len(around))},
        compiler_params=pltpu.CompilerParams(vmem_limit_bytes=56 * 1024 * 1024),
        cost_estimate=pl.CostEstimate(
            flops=(channels + 1) * 12 * 512 * 512 * 1024,
            bytes_accessed=channels * 3 * 1024 * 1024 + 4 * 1024 * 1024,
            transcendentals=0,
        ),
    )(*inputs, *around)


def gather_ring(far):
    return far, to_last(far), to_across(far), to_next(far)


def scatter_ring(outs):
    own, above, across, below = outs
    return own, to_next(above), to_across(across), to_last(below)


def total(parts):
    summed = joined(parts[0], parts[1])
    for part in parts[2:]:
        summed = summed + part.astype(jnp.float32)
    return summed


def relay(above, below):
    return to_last(above[:, :ROWS]), to_next(below[:, ROWS:])


def joined(block, other):
    return block.astype(jnp.float32) + other.astype(jnp.float32)


def scatter_far(outs):
    _, above, low, high, below = outs
    return to_next(low), to_last(high)


def scatter_near(outs, far):
    own, above, _, _, below = outs
    low = jnp.pad(far[0], ((0, 0), (0, ROWS), (0, 0)))
    high = jnp.pad(far[1], ((0, 0), (ROWS, 0), (0, 0)))
    from_below = to_next(joined(above, low).astype(jnp.bfloat16))
    from_above = to_last(joined(below, high).astype(jnp.bfloat16))
    return joined(own, from_below) + from_above.astype(jnp.float32)


def make_tables(place):
    chip = place // 4
    slot = place % 4
    ring = (chip + jnp.arange(RING, dtype=jnp.int32)) % RING
    here = ring[:, None] * 4 + jnp.stack([slot, slot ^ 1])[None, :]
    there = ring[:, None] * 4 + jnp.stack([slot ^ 2, slot ^ 3])[None, :]
    device = jnp.concatenate([here, there]).reshape(-1)
    row_index = (device[:, None] * ROWS + jnp.arange(ROWS, dtype=jnp.int32)[None, :]).reshape(-1)
    owner = jnp.stack([place, place ^ 1])
    freq_index = (owner[:, None] * KEPT + jnp.arange(KEPT, dtype=jnp.int32)[None, :]).reshape(-1)
    cols = jnp.arange(FACTOR_B, dtype=jnp.int32)
    cos_a, sin_a = tables(freq_index, row_index, FACTOR_A)
    fwd_a = jnp.concatenate([cos_a, sin_a], axis=0).astype(jnp.bfloat16)
    cos_b, sin_b = grid_tables()
    cos_t, sin_t = tables(freq_index, cols, FACTOR_A * FACTOR_B)
    return (fwd_a, fwd_a.T, cos_b, sin_b, cos_t, sin_t)


def per_device(streams, short_weight, gate_bias, filter_spectrum):
    place = lax.axis_index("ctx")
    core = place % 2
    channels = streams.shape[1]
    length = streams.shape[2]
    half = channels // 2
    rim = lax.ppermute(streams[:, :, length - LANES :], "ctx", [(i, i + 1) for i in range(15)])

    product = make_product(short_weight, streams, rim)
    rows = product.reshape(channels, ROWS, FACTOR_B)
    kept = lax.dynamic_slice_in_dim(rows, core * half, half, axis=0)
    passed = to_core(lax.dynamic_slice_in_dim(rows, (1 - core) * half, half, axis=0))
    later, passed, swapped = tied(place, passed, filter_spectrum)
    other = to_core(swapped)
    pair = jnp.concatenate([kept, passed], axis=1)

    which = core[None]
    step = CHUNKS[0]
    ring_pieces = len(AROUND)
    far0 = to_far(pair[:step])
    above_o, below_o = to_last(pair), to_next(pair)
    shared = make_tables(later)
    above_o, below_o, shared = tied(above_o, below_o, shared)
    low_o, high_o = relay(above_o, below_o)
    far0, rim, pair = tied(far0, rim, pair)
    pieces = gather_ring(far0)
    gate = make_gate(short_weight, streams, rim)
    around = (pair, above_o, low_o, high_o, below_o)
    far1 = to_far(pair[step:])

    *pieces, far1, gate = tied(*pieces, far1, gate)
    outs0 = convolve(which, (*around, *pieces), 0, filter_spectrum, other, shared, ())
    pieces = gather_ring(far1)
    *pieces, outs0 = tied(*pieces, outs0)
    sum_z0 = total(scatter_ring(outs0[ring_pieces:])).astype(jnp.bfloat16)
    outs1 = convolve(
        which, (*around, *pieces), step, filter_spectrum, other, shared, outs0[:ring_pieces]
    )
    sum_z0, *outs1 = tied(sum_z0, *outs1)
    back0 = to_far(sum_z0)
    sum_z1 = total(scatter_ring(outs1[ring_pieces:])).astype(jnp.bfloat16)
    outs1 = outs1[:ring_pieces]
    low, high, sum_z1, back0 = tied(*scatter_far(outs1), sum_z1, back0)
    back1 = to_far(sum_z1)
    sum_o = scatter_near(outs1, (low, high))
    sums = [
        joined(sum_o[:step], back0).astype(jnp.bfloat16),
        joined(sum_o[step:], back1).astype(jnp.bfloat16),
    ]
    conv = jnp.concatenate(sums, axis=0)
    mine = conv[:, :ROWS]
    swapped = to_core(conv[:, ROWS:])
    conv = jnp.where(
        core == 0, jnp.concatenate([mine, swapped], axis=0), jnp.concatenate([swapped, mine], axis=0)
    )
    conv = conv.reshape(channels, length).astype(jnp.float32)
    direct = gate_bias[:, None] * product.astype(jnp.float32)
    return (gate * (conv + direct)).astype(jnp.bfloat16)


def solution(mesh):
    in_specs = (P(None, "ch", "ctx"), P(None, "ch", None), P("ch"), P(None, "ch", None, "ctx"))
    out_specs = P("ch", "ctx")
    return jax.shard_map(
        per_device, mesh=mesh, in_specs=in_specs, out_specs=out_specs, check_vma=False
    )
```

```python
import math

import jax
import jax.numpy as jnp
import numpy as np
from jax import lax
from jax.experimental import pallas as pl
from jax.experimental.pallas import tpu as pltpu
from jax.sharding import PartitionSpec as P

FACTOR_A = 2048
FACTOR_B = 512
SHORT_TAPS = 3
RING = 4
CHUNKS = (4, 4)
ROWS = 64
KEPT = 128
LANES = 128
COLUMNS = 16384


def send(block, target):
    return lax.ppermute(block, "ctx", [(i, target(i)) for i in range(16)])


def to_core(block):
    return send(block, lambda i: i ^ 1)


def to_far(block):
    return send(block, lambda i: i ^ 2)


def to_next(block):
    return send(block, lambda i: (i + 4) % 16)


def to_last(block):
    return send(block, lambda i: (i - 4) % 16)


def to_across(block):
    return send(block, lambda i: (i + 8) % 16)


def tied(*values):
    return lax.optimization_barrier(values)


def tables(row_index, col_index, size):
    turns = row_index[:, None] * col_index[None, :] % size
    angle = turns.astype(jnp.float32) * (2.0 * math.pi / size)
    return (jnp.cos(angle), -jnp.sin(angle))


def grid_tables():
    index = np.arange(FACTOR_B)
    angle = (index[:, None] * index[None, :] % FACTOR_B) * (2.0 * math.pi / FACTOR_B)
    return jnp.asarray(np.cos(angle), jnp.bfloat16), jnp.asarray(-np.sin(angle), jnp.bfloat16)


def featurize(ref, last_ref, rim_ref, weights):
    last = jnp.where(pl.program_id(0) == 0, rim_ref[0], last_ref[0]).astype(jnp.float32)
    block = ref[0].astype(jnp.float32)
    padded = jnp.concatenate([last, block], axis=1)
    summed = weights[:, 0:1] * block
    for tap in range(1, SHORT_TAPS):
        summed = summed + weights[:, tap : tap + 1] * pltpu.roll(padded, tap, 1)[:, LANES:]
    return summed


def product_kernel(weight_ref, first, first_last, first_rim, third, third_last, third_rim, out):
    left = featurize(first, first_last, first_rim, weight_ref[0].astype(jnp.float32))
    right = featurize(third, third_last, third_rim, weight_ref[2].astype(jnp.float32))
    out[...] = (left * right).astype(jnp.bfloat16)


def gate_kernel(weight_ref, second, second_last, second_rim, out):
    out[...] = featurize(second, second_last, second_rim, weight_ref[1].astype(jnp.float32))


def stream_specs(stream, channels):
    per_step = COLUMNS // LANES
    return [
        pl.BlockSpec((1, channels, COLUMNS), lambda j: (stream, 0, j)),
        pl.BlockSpec((1, channels, LANES), lambda j: (stream, 0, jnp.maximum(j * per_step - 1, 0))),
        pl.BlockSpec((1, channels, LANES), lambda j: (stream, 0, 0)),
    ]


def make_product(weights, streams, rim):
    channels, length = streams.shape[1:]
    return pl.pallas_call(
        product_kernel,
        grid=(length // COLUMNS,),
        in_specs=[pl.BlockSpec(weights.shape, lambda j: (0, 0, 0))]
        + stream_specs(0, channels)
        + stream_specs(2, channels),
        out_specs=pl.BlockSpec((channels, COLUMNS), lambda j: (0, j)),
        out_shape=jax.ShapeDtypeStruct((channels, length), jnp.bfloat16),
        compiler_params=pltpu.CompilerParams(vmem_limit_bytes=56 * 1024 * 1024),
        cost_estimate=pl.CostEstimate(
            flops=14 * channels * length, bytes_accessed=6 * channels * length, transcendentals=0
        ),
    )(weights, streams, streams, rim, streams, streams, rim)


def make_gate(weights, streams, rim):
    channels, length = streams.shape[1:]
    return pl.pallas_call(
        gate_kernel,
        grid=(length // COLUMNS,),
        in_specs=[pl.BlockSpec(weights.shape, lambda j: (0, 0, 0))] + stream_specs(1, channels),
        out_specs=pl.BlockSpec((channels, COLUMNS), lambda j: (0, j)),
        out_shape=jax.ShapeDtypeStruct((channels, length), jnp.float32),
        compiler_params=pltpu.CompilerParams(vmem_limit_bytes=56 * 1024 * 1024),
        cost_estimate=pl.CostEstimate(
            flops=7 * channels * length, bytes_accessed=6 * channels * length, transcendentals=0
        ),
    )(weights, streams, streams, rim)


def dot(left, right):
    return jnp.dot(left, right, preferred_element_type=jnp.float32)


AROUND = (128, 128, 64, 64, 128)
BESIDE = (128, 128, 128, 128)


def conv_kernel(count, core_ref, *refs):
    near, other, fwd_a, inv_a, cos_b, sin_b, cos_ref, sin_ref = refs[count : count + 8]
    half = 2 * KEPT
    block = jnp.concatenate([ref[0] for ref in refs[:count]], axis=0)
    first = dot(fwd_a[...], block)
    cos, sin = cos_ref[...], sin_ref[...]
    real, imag = first[:half], first[half:]
    mid_real = (real * cos - imag * sin).astype(jnp.bfloat16)
    mid_imag = (real * sin + imag * cos).astype(jnp.bfloat16)
    real = dot(mid_real, cos_b[...]) - dot(mid_imag, sin_b[...])
    imag = dot(mid_real, sin_b[...]) + dot(mid_imag, cos_b[...])
    filter_real = jnp.concatenate([near[0, 0].T, other[0, 0].T], axis=0)
    filter_imag = jnp.concatenate([near[1, 0].T, other[1, 0].T], axis=0)
    prod_real = (real * filter_real - imag * filter_imag).astype(jnp.bfloat16)
    prod_imag = (real * filter_imag + imag * filter_real).astype(jnp.bfloat16)
    real = dot(prod_real, cos_b[...]) + dot(prod_imag, sin_b[...])
    imag = dot(prod_imag, cos_b[...]) - dot(prod_real, sin_b[...])
    turn = jnp.concatenate(
        [
            (real * cos + imag * sin).astype(jnp.bfloat16),
            (imag * cos - real * sin).astype(jnp.bfloat16),
        ],
        axis=0,
    )
    scale = 1.0 / (FACTOR_A * FACTOR_B)
    begin = 0
    for out in refs[-count:]:
        rows = out.shape[1]
        out[0] = (dot(inv_a[begin : begin + rows], turn) * scale).astype(jnp.bfloat16)
        begin += rows


def convolve(core, pieces, begin, near, other, shared, around):
    half = near.shape[1] // 2
    channels = pieces[-1].shape[0]
    count = len(pieces)

    def spec(rows, first):
        return pl.BlockSpec((1, rows, FACTOR_B), lambda c, core: (first + c, 0, 0))

    specs = [spec(rows, begin) for rows in AROUND] + [spec(rows, 0) for rows in BESIDE]
    shapes = [(half, rows, FACTOR_B) for rows in AROUND]
    shapes += [(channels, rows, FACTOR_B) for rows in BESIDE]
    spectrum = (2, 1, FACTOR_B, KEPT)
    filters = pl.BlockSpec(spectrum, lambda c, core: (0, core[0] * half + begin + c, 0, 0))
    whole = [pl.BlockSpec(memory_space=pltpu.VMEM) for table in shared]
    inputs = (core, *pieces, near, other, *shared)
    return pl.pallas_call(
        lambda *refs: conv_kernel(count, *refs),
        grid_spec=pltpu.PrefetchScalarGridSpec(
            num_scalar_prefetch=1,
            grid=(channels,),
            in_specs=specs
            + [filters, filters]
            + whole
            + [pl.BlockSpec(memory_space=pl.ANY) for out in around],
            out_specs=specs,
        ),
        out_shape=[jax.ShapeDtypeStruct(shape, jnp.bfloat16) for shape in shapes],
        input_output_aliases={len(inputs) + i: i for i in range(len(around))},
        compiler_params=pltpu.CompilerParams(vmem_limit_bytes=56 * 1024 * 1024),
        cost_estimate=pl.CostEstimate(
            flops=(channels + 1) * 12 * 512 * 512 * 1024,
            bytes_accessed=channels * 3 * 1024 * 1024 + 4 * 1024 * 1024,
            transcendentals=0,
        ),
    )(*inputs, *around)


def gather_ring(far):
    return far, to_last(far), to_across(far), to_next(far)


def scatter_ring(outs):
    own, above, across, below = outs
    return own, to_next(above), to_across(across), to_last(below)


def total(parts):
    summed = joined(parts[0], parts[1])
    for part in parts[2:]:
        summed = summed + part.astype(jnp.float32)
    return summed


def relay(above, below):
    return to_last(above[:, :ROWS]), to_next(below[:, ROWS:])


def joined(block, other):
    return block.astype(jnp.float32) + other.astype(jnp.float32)


def scatter_far(outs):
    _, above, low, high, below = outs
    return to_next(low), to_last(high)


def scatter_near(outs, far):
    own, above, _, _, below = outs
    low = jnp.pad(far[0], ((0, 0), (0, ROWS), (0, 0)))
    high = jnp.pad(far[1], ((0, 0), (ROWS, 0), (0, 0)))
    from_below = to_next(joined(above, low).astype(jnp.bfloat16))
    from_above = to_last(joined(below, high).astype(jnp.bfloat16))
    return joined(own, from_below) + from_above.astype(jnp.float32)


def make_tables(place):
    chip = place // 4
    slot = place % 4
    ring = (chip + jnp.arange(RING, dtype=jnp.int32)) % RING
    here = ring[:, None] * 4 + jnp.stack([slot, slot ^ 1])[None, :]
    there = ring[:, None] * 4 + jnp.stack([slot ^ 2, slot ^ 3])[None, :]
    device = jnp.concatenate([here, there]).reshape(-1)
    row_index = (device[:, None] * ROWS + jnp.arange(ROWS, dtype=jnp.int32)[None, :]).reshape(-1)
    owner = jnp.stack([place, place ^ 1])
    freq_index = (owner[:, None] * KEPT + jnp.arange(KEPT, dtype=jnp.int32)[None, :]).reshape(-1)
    cols = jnp.arange(FACTOR_B, dtype=jnp.int32)
    cos_a, sin_a = tables(freq_index, row_index, FACTOR_A)
    fwd_a = jnp.concatenate([cos_a, sin_a], axis=0).astype(jnp.bfloat16)
    cos_b, sin_b = grid_tables()
    cos_t, sin_t = tables(freq_index, cols, FACTOR_A * FACTOR_B)
    return (fwd_a, fwd_a.T, cos_b, sin_b, cos_t, sin_t)


def per_device(streams, short_weight, gate_bias, filter_spectrum):
    place = lax.axis_index("ctx")
    core = place % 2
    channels = streams.shape[1]
    length = streams.shape[2]
    half = channels // 2
    rim = lax.ppermute(streams[:, :, length - LANES :], "ctx", [(i, i + 1) for i in range(15)])

    product = make_product(short_weight, streams, rim)
    rows = product.reshape(channels, ROWS, FACTOR_B)
    kept = lax.dynamic_slice_in_dim(rows, core * half, half, axis=0)
    passed = to_core(lax.dynamic_slice_in_dim(rows, (1 - core) * half, half, axis=0))
    later, passed, swapped = tied(place, passed, filter_spectrum)
    other = to_core(swapped)
    pair = jnp.concatenate([kept, passed], axis=1)

    which = core[None]
    step = CHUNKS[0]
    ring_pieces = len(AROUND)
    far0 = to_far(pair[:step])
    above_o, below_o = to_last(pair), to_next(pair)
    shared = make_tables(later)
    above_o, below_o, shared, far0, rim, pair = tied(
        above_o, below_o, shared, far0, rim, pair
    )
    low_o, high_o = relay(above_o, below_o)
    pieces = gather_ring(far0)
    gate = make_gate(short_weight, streams, rim)
    around = (pair, above_o, low_o, high_o, below_o)
    far1 = to_far(pair[step:])

    *pieces, far1, gate = tied(*pieces, far1, gate)
    outs0 = convolve(which, (*around, *pieces), 0, filter_spectrum, other, shared, ())
    pieces = gather_ring(far1)
    *pieces, outs0 = tied(*pieces, outs0)
    sum_z0 = total(scatter_ring(outs0[ring_pieces:])).astype(jnp.bfloat16)
    outs1 = convolve(
        which, (*around, *pieces), step, filter_spectrum, other, shared, outs0[:ring_pieces]
    )
    sum_z0, *outs1 = tied(sum_z0, *outs1)
    back0 = to_far(sum_z0)
    sum_z1 = total(scatter_ring(outs1[ring_pieces:])).astype(jnp.bfloat16)
    outs1 = outs1[:ring_pieces]
    low, high, sum_z1, back0 = tied(*scatter_far(outs1), sum_z1, back0)
    back1 = to_far(sum_z1)
    sum_o = scatter_near(outs1, (low, high))
    sums = [
        joined(sum_o[:step], back0).astype(jnp.bfloat16),
        joined(sum_o[step:], back1).astype(jnp.bfloat16),
    ]
    conv = jnp.concatenate(sums, axis=0)
    mine = conv[:, :ROWS]
    swapped = to_core(conv[:, ROWS:])
    conv = jnp.where(
        core == 0, jnp.concatenate([mine, swapped], axis=0), jnp.concatenate([swapped, mine], axis=0)
    )
    conv = conv.reshape(channels, length).astype(jnp.float32)
    direct = gate_bias[:, None] * product.astype(jnp.float32)
    return (gate * (conv + direct)).astype(jnp.bfloat16)


def solution(mesh):
    in_specs = (P(None, "ch", "ctx"), P(None, "ch", None), P("ch"), P(None, "ch", None, "ctx"))
    out_specs = P("ch", "ctx")
    return jax.shard_map(
        per_device, mesh=mesh, in_specs=in_specs, out_specs=out_specs, check_vma=False
    )
```
